256 devices in a mesh: dp: 32 (over x, z_hi, core), tensor: 8 (over z_lo, y).
Axes of the slice: x: 4, y: 4, z: 8 (z_hi: 4, z_lo: 2; z = z_hi * 2 + z_lo), core: 2. Of those that a mesh axis runs over, the one named last changes fastest.
Arguments:
- queries: bfloat16 [16384, 4096], P('dp', 'tensor'), may hold values from -14 to 14
- key_rows: bfloat16 [16384, 1024], P('dp', 'tensor'), may hold values from -4.5 to 4.5
- value_rows: bfloat16 [16384, 1024], P('dp', 'tensor'), may hold values from -6 to 6
- grad_out: bfloat16 [16384, 4096], P('dp', 'tensor'), may hold values from -6 to 6
- out_weight: bfloat16 [4096, 4096], P('tensor'), may hold values from -0.09375 to 0.09375
- lengths: int32 [64], replicated, may hold values from 1 to 2048, 16384 in all
Outputs:
- projected: bfloat16 [16384, 4096], P(('dp', 'tensor'))
- grad_queries: bfloat16 [16384, 4096], P('dp', 'tensor')
- grad_keys: bfloat16 [16384, 1024], P('dp', 'tensor')
- grad_values: bfloat16 [16384, 1024], P('dp', 'tensor')
The draws below stay inside these ranges and needn't reach their ends.
Inputs may be any that keep to these rules, and one draw needn't show every extreme that they name: The lengths sum to 16384; the longest document has exactly 2048 tokens.
All inputs are finite; a program needn't handle non-finite values.
Results may differ from the reference program's by a relative error of at most 0.035.
Values may be sent and summed in bfloat16 or wider, within the bound.
No kernel may reach another device: no remote copies, remote signals or barrier semaphores. Data moves between devices by JAX's collectives and lax.ppermute only.
A program may use at most 128 MiB of HBM per device.

```python
import math
import jax
import jax.numpy as jnp
import numpy as np
from jax import lax

HEAD_DIM = 128
HQ_DEV = 4
OUT_FEATURES = 4096
REACH = 4
TOK_DEV = 512
KV_HEADS = 8
HEADS = 32
LENGTH = 16384
MOST = 2048
DOCS = 64
N_DP = 32


def draw_key_rows(key, part):
    key = jax.random.fold_in(key, 5)
    return jax.random.truncated_normal(key, -4.0, 4.0, (LENGTH, KV_HEADS * HEAD_DIM)).astype(jnp.bfloat16)


def draw_queries(key, part):
    key = jax.random.fold_in(key, 7)
    return jax.random.truncated_normal(key, -4.0, 4.0, (LENGTH, HEADS * HEAD_DIM)).astype(jnp.bfloat16)


def block_levels(key, shape, cuts, least, top_value):
    loudness, own = 1.0, jax.random.fold_in(key, 6)
    for position, parts in cuts:
        steps = jnp.exp(jax.random.uniform(jax.random.fold_in(own, position), (parts,), jnp.float32, least / len(cuts), top_value / len(cuts)))
        loudness = loudness * jnp.repeat(steps, shape[position] // parts).reshape([-1 if axis == position else 1 for axis in range(len(shape))])
    return loudness


def profile(amount, total, limit, skew):
    weights = [(1 << 20) // math.isqrt(grade ** skew) + 1 for grade in range(2, amount + 1)]
    rest, holding = total - limit - (amount - 1), [1] * (amount - 1)
    while rest > 0:
        free = [i for i in range(amount - 1) if holding[i] < limit]
        pool, left = sum([weights[i] for i in free]), rest
        for i in free:
            extra = min(limit - holding[i], max(1, left * weights[i] // pool), rest)
            holding[i] = holding[i] + extra
            rest = rest - extra
    return np.array([limit] + holding)


def ragged_sizes(key, count, total, limit, skew):
    if count == 2:
        one = jax.random.randint(key, (), max(1, total - limit), min(limit, total - 1) + 1)
        return jnp.stack([one, total - one])
    tallies = jnp.asarray(profile(count, total, limit, skew), jnp.int32)
    couples = (count - 1) // 2
    source_of, sink = tallies[1:1 + 2 * couples:2], tallies[2:2 + 2 * couples:2]
    room = jnp.minimum(source_of - 1, limit - sink)
    passed = jax.random.randint(jax.random.fold_in(key, 1), (couples,), 0, 1 << 20) % (room + 1)
    tallies = tallies.at[1:1 + 2 * couples:2].set(source_of - passed).at[2:2 + 2 * couples:2].set(sink + passed)
    return tallies[jax.random.permutation(jax.random.fold_in(key, 2), count)]


def noise(key, shape, width, limit, split=(), kind=jnp.bfloat16):
    drawn = jax.random.normal(key, shape, jnp.float32) * width
    if len(split) > 0:
        drawn = block_levels(key, shape, split, -0.22, 0.18) * drawn
    return jnp.clip(drawn, min=-limit, max=limit).astype(kind)


def setup_inputs(seed: int = 0) -> dict:
    splits = jax.random.split(jax.random.key(seed), 7)
    return {
        "queries": draw_queries(jax.random.fold_in(splits[6], 71), 0),
        "key_rows": draw_key_rows(jax.random.fold_in(splits[6], 71), 0),
        "value_rows": noise(splits[2], (LENGTH, KV_HEADS * HEAD_DIM), 1.0, 6.0, ((0, 32), (1, 8))),
        "grad_out": noise(splits[3], (LENGTH, HEADS * HEAD_DIM), 1.0, 6.0, ((0, 32), (1, 8))),
        "out_weight": noise(splits[4], (HEADS * HEAD_DIM, OUT_FEATURES), (HEADS * HEAD_DIM) ** -0.5, 0.09375, ((0, 8),)),
        "lengths": ragged_sizes(splits[5], DOCS, LENGTH, MOST, 2).astype(jnp.int32),
    }


NEG_BIG = -1e30


def doc_starts(lengths, positions):
    ends_at = jnp.cumsum(lengths).astype(jnp.int32)
    before = ends_at[None, :] <= positions[:, None]
    return jnp.sum(jnp.where(before, lengths[None, :], 0), axis=1).astype(jnp.int32)


def block_terms(query_heads, grad_heads, key_win, value_win, query_pos, key_pos, query_start):
    scaling = HEAD_DIM ** -0.5
    live_mask = (key_pos[None, :] >= query_start[:, None]) & (key_pos[None, :] <= query_pos[:, None])
    query_f = query_heads.astype(jnp.float32)
    grad_f = grad_heads.astype(jnp.float32)
    key_f = key_win.astype(jnp.float32)
    value_f = value_win.astype(jnp.float32)
    scores = scaling * jnp.einsum("rhd,cd->hrc", query_f, key_f)
    scores = jnp.where(live_mask[None], scores, NEG_BIG)
    row_max = jnp.max(scores, axis=-1, keepdims=True)
    row_sum = jnp.sum(jnp.where(live_mask[None], jnp.exp(scores - row_max), 0.0), axis=-1, keepdims=True)
    log_norm = row_max + jnp.log(row_sum)
    attn_probs = jnp.where(live_mask[None], jnp.exp(scores - log_norm), 0.0)
    probs_half = lax.optimization_barrier(attn_probs.astype(jnp.bfloat16)).astype(jnp.float32)
    attn_acc = jnp.einsum("hrc,cd->rhd", probs_half, value_f)
    attn_out = attn_acc.astype(jnp.bfloat16)
    grad_probs = jnp.einsum("rhd,cd->hrc", grad_f, value_f)
    row_delta = jnp.sum(grad_f * attn_acc, axis=-1).transpose(1, 0)[..., None]
    grad_scores = lax.optimization_barrier((attn_probs * (grad_probs - row_delta)).astype(jnp.bfloat16)).astype(jnp.float32)
    grad_query = scaling * jnp.einsum("hrc,cd->rhd", grad_scores, key_f)
    grad_key = scaling * jnp.einsum("hrc,rhd->cd", grad_scores, query_f)
    grad_value = jnp.einsum("hrc,rhd->cd", probs_half, grad_f)
    row_count = query_heads.shape[0]
    return (attn_out.reshape(row_count, HQ_DEV * HEAD_DIM), grad_query.reshape(row_count, HQ_DEV * HEAD_DIM), grad_key, grad_value)


def reference(queries, key_rows, value_rows, grad_out, out_weight, lengths):
    window = (REACH + 1) * TOK_DEV
    group_width = HQ_DEV * HEAD_DIM
    zero_rows = jnp.zeros((REACH * TOK_DEV, KV_HEADS * HEAD_DIM), jnp.bfloat16)
    keys_pad = jnp.concatenate([zero_rows, key_rows], axis=0)
    values_pad = jnp.concatenate([zero_rows, value_rows], axis=0)

    def per_block(block_id):
        row_first = (block_id * TOK_DEV).astype(jnp.int32)
        query_pos = row_first + jnp.arange(TOK_DEV, dtype=jnp.int32)
        key_pos = row_first - REACH * TOK_DEV + jnp.arange(window, dtype=jnp.int32)
        query_start = doc_starts(lengths, query_pos)

        def per_group(group_id):
            column = (group_id * group_width).astype(jnp.int32)
            kv_column = (group_id * HEAD_DIM).astype(jnp.int32)
            query_block = lax.dynamic_slice(queries, (row_first, column), (TOK_DEV, group_width)).reshape(TOK_DEV, HQ_DEV, HEAD_DIM)
            grad_block = lax.dynamic_slice(grad_out, (row_first, column), (TOK_DEV, group_width)).reshape(TOK_DEV, HQ_DEV, HEAD_DIM)
            key_win = lax.dynamic_slice(keys_pad, (row_first, kv_column), (window, HEAD_DIM))
            value_win = lax.dynamic_slice(values_pad, (row_first, kv_column), (window, HEAD_DIM))
            return block_terms(query_block, grad_block, key_win, value_win, query_pos, key_pos, query_start)

        return lax.map(per_group, jnp.arange(KV_HEADS, dtype=jnp.int32))

    attn_all, grad_q_all, grad_k_all, grad_v_all = lax.map(per_block, jnp.arange(N_DP, dtype=jnp.int32))
    attn_out = attn_all.transpose(0, 2, 1, 3).reshape(LENGTH, HEADS * HEAD_DIM)
    grad_queries = grad_q_all.transpose(0, 2, 1, 3).reshape(LENGTH, HEADS * HEAD_DIM).astype(jnp.bfloat16)
    key_tiles = grad_k_all.reshape(N_DP, KV_HEADS, REACH + 1, TOK_DEV, HEAD_DIM)
    value_tiles = grad_v_all.reshape(N_DP, KV_HEADS, REACH + 1, TOK_DEV, HEAD_DIM)
    key_pad = jnp.zeros((N_DP + REACH, TOK_DEV, KV_HEADS, HEAD_DIM), jnp.float32)
    value_pad = jnp.zeros((N_DP + REACH, TOK_DEV, KV_HEADS, HEAD_DIM), jnp.float32)
    for tile_id in range(REACH + 1):
        key_pad = key_pad.at[tile_id:tile_id + N_DP].add(key_tiles[:, :, tile_id].transpose(0, 2, 1, 3))
        value_pad = value_pad.at[tile_id:tile_id + N_DP].add(value_tiles[:, :, tile_id].transpose(0, 2, 1, 3))
    grad_keys = key_pad[REACH:].reshape(LENGTH, KV_HEADS * HEAD_DIM).astype(jnp.bfloat16)
    grad_values = value_pad[REACH:].reshape(LENGTH, KV_HEADS * HEAD_DIM).astype(jnp.bfloat16)
    summed = jnp.zeros((LENGTH, OUT_FEATURES), jnp.float32)
    for group_id in range(KV_HEADS):
        part_sum = jnp.dot(attn_out[:, group_id * group_width:(group_id + 1) * group_width], out_weight[group_id * group_width:(group_id + 1) * group_width], preferred_element_type=jnp.float32).astype(jnp.bfloat16)
        summed = summed + lax.optimization_barrier(part_sum).astype(jnp.float32)
    projected = summed.astype(jnp.bfloat16)
    return (projected, grad_queries, grad_keys, grad_values)
```

```python
import functools
import math

import jax
import jax.numpy as jnp
from jax import lax
from jax.experimental import pallas as pl
from jax.experimental.pallas import tpu as pltpu
from jax.sharding import PartitionSpec as P

HEAD = 128
HEADS_DEV = 4
REACH = 4
ROWS = 512
UNIT = 64
COLS = UNIT * HEADS_DEV
UNITS = ROWS // UNIT
CONTEXT = (REACH + 1) * ROWS
KEYS = 256
NEG_BIG = -1e30
SCALE = HEAD**-0.5
SCALE_LOG2 = SCALE * math.log2(math.e)
NT = (((1,), (1,)), ((), ()))
NN = (((1,), (0,)), ((), ()))


def dot(a, b, dims=NN):
    return lax.dot_general(a, b, dims, preferred_element_type=jnp.float32)


def fill_context(par, own, near, near_twin, far, twin, ctx, sems):
    slots = [(far, 0), (near, 2), (own, 4), (near_twin, 3 - 2 * par), (twin, 1 + 2 * par)]
    copies = []
    for number, (source, slot) in enumerate(slots):
        first = slot * ROWS
        if not isinstance(first, int):
            first = pl.multiple_of(first, ROWS)
        copies.append(pltpu.make_async_copy(source, ctx.at[pl.ds(first, ROWS)], sems.at[number]))
    for copy in copies:
        copy.start()
    for copy in copies:
        copy.wait()


def stacked(ref, row0):
    return jnp.concatenate(
        [ref[pl.ds(row0, UNIT), h * HEAD : (h + 1) * HEAD] for h in range(HEADS_DEV)], axis=0
    )


def masked(scores, first_key, start, row):
    key = first_key + lax.broadcasted_iota(jnp.int32, scores.shape, 0)
    return jnp.where((key >= start) & (key <= row), scores, NEG_BIG)


def unit_rows(j):
    lane = lax.broadcasted_iota(jnp.int32, (1, COLS), 1)
    return REACH * ROWS + j * UNIT + (lane & (UNIT - 1))


def over_keys(sc, j, block):
    lowest, highest = sc[8 + j], sc[16 + j]
    first_row = REACH * ROWS + j * UNIT
    begin = lowest // KEYS
    end = (first_row + UNIT - 1) // KEYS + 1

    @pl.loop(begin, end)
    def _(kb):
        first_key = pl.multiple_of(kb * KEYS, KEYS)
        whole = (first_key >= highest) & (first_key + KEYS - 1 <= first_row)

        @pl.when(whole)
        def _():
            block(first_key, False)

        @pl.when(jnp.logical_not(whole))
        def _():
            block(first_key, True)


def forward_kernel(
    sc, starts, q, g, own, near, near_twin, far, twin, attn, norm, delta, ctx, vt, top, total, acc, sems
):
    par, y, zl = sc[0], sc[1], sc[2]
    fill_context(par, own, near, near_twin, far, twin, ctx, sems)
    for tile in range(REACH + 1):

        @pl.when((tile + 1) * ROWS > sc[8])
        def _():
            here = slice(tile * ROWS, (tile + 1) * ROWS)
            vt[:, here] = ctx[here, HEAD:].T

    @pl.loop(0, UNITS)
    def _(i):
        j = (zl ^ (i & 1)) * 4 + ((y + (i >> 1)) & 3)
        row0 = pl.multiple_of(j * UNIT, UNIT)
        q_unit = stacked(q, row0)
        start, row = starts[pl.ds(j, 1), :], unit_rows(j)
        top[...] = jnp.full((1, COLS), NEG_BIG, jnp.float32)
        total[...] = jnp.zeros((1, COLS), jnp.float32)
        acc[...] = jnp.zeros((HEAD, COLS), jnp.float32)

        def block(first_key, needs_mask):
            s = dot(ctx[pl.ds(first_key, KEYS), :HEAD], q_unit, NT) * SCALE_LOG2
            if needs_mask:
                s = masked(s, first_key, start, row)
            old = top[...]
            new = jnp.maximum(old, jnp.max(s, axis=0, keepdims=True))
            p = jnp.exp2(s - new)
            shrink = jnp.exp2(old - new)
            top[...] = new
            total[...] = total[...] * shrink + jnp.sum(p, axis=0, keepdims=True)
            acc[...] = acc[...] * shrink + dot(vt[:, pl.ds(first_key, KEYS)], p.astype(jnp.bfloat16))

        over_keys(sc, j, block)
        out = acc[...] / total[...]
        norm[pl.ds(j, 1), :] = top[...] + jnp.log2(total[...])
        g_unit = stacked(g, row0).astype(jnp.float32).T
        delta[pl.ds(j, 1), :] = jnp.sum(out * g_unit, axis=0, keepdims=True)
        flat = out.T.astype(jnp.bfloat16)
        place = pl.multiple_of(i * UNIT, UNIT)
        for h in range(HEADS_DEV):
            attn[pl.ds(place, UNIT), h * HEAD : (h + 1) * HEAD] = flat[h * UNIT : (h + 1) * UNIT]


def backward_kernel(
    sc, starts, norm, delta, q, g, own, near, near_twin, far, twin, gq, mine, given, ctx, kt, dkv, dq, sems
):
    par = sc[0]
    fill_context(par, own, near, near_twin, far, twin, ctx, sems)
    for tile in range(REACH + 1):
        here = slice(tile * ROWS, (tile + 1) * ROWS)
        dkv[here, :] = jnp.zeros((ROWS, 2 * HEAD), jnp.float32)

        @pl.when((tile + 1) * ROWS > sc[8])
        def _():
            kt[:, here] = ctx[here, :HEAD].T

    @pl.loop(0, UNITS)
    def _(j):
        row0 = pl.multiple_of(j * UNIT, UNIT)
        q_unit, g_unit = stacked(q, row0), stacked(g, row0)
        start, row = starts[pl.ds(j, 1), :], unit_rows(j)
        norm_unit, delta_unit = norm[pl.ds(j, 1), :], delta[pl.ds(j, 1), :]
        dq[...] = jnp.zeros((HEAD, COLS), jnp.float32)

        def block(first_key, needs_mask):
            here = pl.ds(first_key, KEYS)
            s = dot(ctx[here, :HEAD], q_unit, NT) * SCALE_LOG2
            if needs_mask:
                s = masked(s, first_key, start, row)
            p = jnp.exp2(s - norm_unit)
            dp = dot(ctx[here, HEAD:], g_unit, NT)
            ds = (p * (dp - delta_unit)).astype(jnp.bfloat16)
            dkv[here, :HEAD] += dot(ds, q_unit)
            dkv[here, HEAD:] += dot(p.astype(jnp.bfloat16), g_unit)
            dq[...] += dot(kt[:, here], ds)

        over_keys(sc, j, block)
        flat = (dq[...] * SCALE).T.astype(jnp.bfloat16)
        for h in range(HEADS_DEV):
            gq[pl.ds(row0, UNIT), h * HEAD : (h + 1) * HEAD] = flat[h * UNIT : (h + 1) * UNIT]

    def tile_out(slot):
        here = pl.ds(pl.multiple_of(slot * ROWS, ROWS), ROWS)
        return jnp.concatenate([dkv[here, :HEAD] * SCALE, dkv[here, HEAD:]], axis=1).astype(jnp.bfloat16)

    for number in range(3):
        mine[number] = tile_out(2 * number)
    given[0] = tile_out(1 + 2 * par)
    given[1] = tile_out(3 - 2 * par)


VMEM = pl.BlockSpec(memory_space=pltpu.VMEM)
SMEM = pl.BlockSpec(memory_space=pltpu.SMEM)
ANY = pl.BlockSpec(memory_space=pl.ANY)


def forward(sc, starts, q, g, tiles):
    stat = jax.ShapeDtypeStruct((UNITS, COLS), jnp.float32)
    return pl.pallas_call(
        forward_kernel,
        out_shape=(jax.ShapeDtypeStruct(q.shape, jnp.bfloat16), stat, stat),
        in_specs=[SMEM] + [VMEM] * 3 + [ANY] * 5,
        out_specs=(VMEM, VMEM, VMEM),
        scratch_shapes=[
            pltpu.VMEM((CONTEXT, 2 * HEAD), jnp.bfloat16),
            pltpu.VMEM((HEAD, CONTEXT), jnp.bfloat16),
            pltpu.VMEM((1, COLS), jnp.float32),
            pltpu.VMEM((1, COLS), jnp.float32),
            pltpu.VMEM((HEAD, COLS), jnp.float32),
            pltpu.SemaphoreType.DMA((5,)),
        ],
        compiler_params=pltpu.CompilerParams(vmem_limit_bytes=40 * 2**20),
        cost_estimate=pl.CostEstimate(flops=4 * 10**9, bytes_accessed=3 * 2**20, transcendentals=4 * 10**6),
        name="attention_forward",
    )(sc, starts, q, g, *tiles)


def backward(sc, starts, norm, delta, q, g, tiles):
    return pl.pallas_call(
        backward_kernel,
        out_shape=(
            jax.ShapeDtypeStruct(q.shape, jnp.bfloat16),
            jax.ShapeDtypeStruct((3, ROWS, 2 * HEAD), jnp.bfloat16),
            jax.ShapeDtypeStruct((2, ROWS, 2 * HEAD), jnp.bfloat16),
        ),
        in_specs=[SMEM] + [VMEM] * 5 + [ANY] * 5,
        out_specs=(VMEM, VMEM, VMEM),
        scratch_shapes=[
            pltpu.VMEM((CONTEXT, 2 * HEAD), jnp.bfloat16),
            pltpu.VMEM((HEAD, CONTEXT), jnp.bfloat16),
            pltpu.VMEM((CONTEXT, 2 * HEAD), jnp.float32),
            pltpu.VMEM((HEAD, COLS), jnp.float32),
            pltpu.SemaphoreType.DMA((5,)),
        ],
        compiler_params=pltpu.CompilerParams(vmem_limit_bytes=40 * 2**20),
        cost_estimate=pl.CostEstimate(flops=10**10, bytes_accessed=6 * 2**20, transcendentals=4 * 10**6),
        name="attention_backward",
    )(sc, starts, norm, delta, q, g, *tiles)


def shifted(x, distance):
    n = lax.axis_size("dp")
    return lax.ppermute(x, "dp", [(i, i + distance) for i in range(n) if 0 <= i + distance < n])


def twinned(x):
    return lax.ppermute(x, "dp", [(i, i ^ 1) for i in range(lax.axis_size("dp"))])


def along_y(x, step):
    return lax.ppermute(x, "tensor", [(i, (i & 4) | ((i + step) & 3)) for i in range(8)])


def across_z(x):
    return lax.ppermute(x, "tensor", [(i, i ^ 4) for i in range(8)])


def half(x):
    return x.astype(jnp.bfloat16)


def wide(x):
    return x.astype(jnp.float32)


def on_device(queries, key_rows, value_rows, grad_out, out_weight, lengths):
    dp, tensor = lax.axis_index("dp"), lax.axis_index("tensor")
    par = dp & 1
    odd = par == 1
    own = jnp.concatenate([key_rows, value_rows], axis=1)
    near = shifted(own, 2)
    near_twin = twinned(near)
    far = shifted(near, 2)
    twin = twinned(jnp.where(odd, far, own))
    tiles = (own, near, near_twin, far, twin)

    base = (dp - REACH) * ROWS
    position = dp * ROWS + jnp.arange(ROWS, dtype=jnp.int32)
    ends = jnp.cumsum(lengths)
    start = jnp.max(jnp.where(ends[None, :] <= position[:, None], ends[None, :], 0), axis=1) - base
    start = start.reshape(UNITS, UNIT)
    head = jnp.stack([par, tensor & 3, tensor >> 2] + [jnp.int32(0)] * 5)
    sc = jnp.concatenate([head, start[:, 0], start[:, -1]]).astype(jnp.int32)
    starts = jnp.tile(start, (1, HEADS_DEV)).astype(jnp.int32)

    attn, norm, delta = forward(sc, starts, queries, grad_out, tiles)

    block = 2 * UNIT
    cut = out_weight.shape[1] // 2
    opposite = half(dot(attn[2 * block : 3 * block], out_weight))
    from_left = along_y(opposite[:, :cut], 1)
    from_right = along_y(opposite[:, cut:], -1)
    after = half(dot(attn[block : 2 * block], out_weight))
    before = half(dot(attn[3 * block :], out_weight))
    here = half(dot(attn[:block], out_weight))
    gq, mine, given = backward(sc, starts, norm, delta, queries, grad_out, tiles)
    after = jnp.concatenate([half(wide(after[:, :cut]) + wide(from_left)), after[:, cut:]], axis=1)
    before = jnp.concatenate([before[:, :cut], half(wide(before[:, cut:]) + wide(from_right))], axis=1)
    here = wide(here) + wide(along_y(after, 1)) + wide(along_y(before, -1))
    projected = half(here[:UNIT] + wide(across_z(half(here[UNIT:]))))

    got = wide(twinned(given))
    far_sum = half(wide(mine[0]) + jnp.where(odd, got[0], 0.0))
    near_sum = wide(mine[1]) + got[1]
    own_sum = wide(mine[2]) + jnp.where(odd, 0.0, got[0])
    near_sum = half(near_sum + wide(shifted(far_sum, -2)))
    own_sum = half(own_sum + wide(shifted(near_sum, -2)))
    return projected, gq, own_sum[:, :HEAD], own_sum[:, HEAD:]


def solution(mesh):
    split = P("dp", "tensor")
    return jax.shard_map(
        on_device,
        mesh=mesh,
        in_specs=(split, split, split, split, P("tensor", None), P()),
        out_specs=(P(("dp", "tensor"), None), split, split, split),
        check_vma=False,
    )
```

```python
import math

import jax
import jax.numpy as jnp
from jax import lax
from jax.experimental import pallas as pl
from jax.experimental.pallas import tpu as pltpu
from jax.sharding import PartitionSpec as P

HEAD = 128
HEADS_DEV = 4
REACH = 4
FAR = 2
ROWS = 512
BLOCK = 64
UNIT = 256
COLS = UNIT * HEADS_DEV
UNITS = ROWS // UNIT
KEYS = 512
NEG_BIG = -1e30
SCALE = HEAD**-0.5
SCALE_LOG2 = SCALE * math.log2(math.e)
NT = (((1,), (1,)), ((), ()))
NN = (((1,), (0,)), ((), ()))


def dot(a, b, dims=NN):
    return lax.dot_general(a, b, dims, preferred_element_type=jnp.float32)


def fetch(pieces, kc, vc, whole, sems, meanwhile=lambda: None):
    copies = [pltpu.make_async_copy(*pair, sems.at[10 + i]) for i, pair in enumerate(whole)]
    for number, (tile, slot) in enumerate(pieces):
        first = slot * ROWS
        here = pl.ds(first if isinstance(first, int) else pl.multiple_of(first, ROWS), ROWS)
        copies.append(pltpu.make_async_copy(tile.at[0], kc.at[here], sems.at[2 * number]))
        copies.append(pltpu.make_async_copy(tile.at[1], vc.at[here], sems.at[2 * number + 1]))
    for copy in copies:
        copy.start()
    meanwhile()
    for copy in copies:
        copy.wait()


def near_pieces(par, own, near, twin_own, near_twin):
    return [(near, 0), (own, 2), (twin_own, 3 - 2 * par), (near_twin, 1 + 2 * par)]


def before_pieces(par, near, twin_own, near_twin, far, far_twin):
    return [(far, 0), (near, 2), (near_twin, 3 - 2 * par), (far_twin, 1 + 3 * par), (twin_own, 4 - par)]


def far_pieces(par, far, far_twin, near_twin):
    return [(far, 0), (far_twin, 1 + par), (near_twin, 2 - par)]


def stacked(ref, row0):
    return jnp.concatenate(
        [ref[pl.ds(row0, UNIT), h * HEAD : (h + 1) * HEAD] for h in range(HEADS_DEV)], axis=0
    )


def masked(scores, first_key, start, row):
    key = first_key + lax.broadcasted_iota(jnp.int32, scores.shape, 0)
    return jnp.where((key >= start) & (key <= row), scores, NEG_BIG)


def unit_rows(j):
    lane = lax.broadcasted_iota(jnp.int32, (1, COLS), 1)
    return REACH * ROWS + j * UNIT + (lane & (UNIT - 1))


def over_keys(sc, j, tiles, keys, block):
    lowest, highest = sc[3 + j], sc[3 + UNITS + j]
    first_row = REACH * ROWS + j * UNIT
    begin = jnp.maximum(lowest, tiles[0] * ROWS) // keys
    end = jnp.minimum((first_row + UNIT - 1) // keys + 1, (tiles[-1] + 1) * ROWS // keys)

    @pl.loop(begin, end)
    def _(kb):
        first_key = pl.multiple_of(kb * keys, keys)
        whole = (first_key >= highest) & (first_key + keys - 1 <= first_row)

        @pl.when(whole)
        def _():
            block(first_key, False)

        @pl.when(jnp.logical_not(whole))
        def _():
            block(first_key, True)


def transposed(sc, tiles, source, target):
    for slot, tile in enumerate(tiles):

        @pl.when((tile + 1) * ROWS > sc[3])
        def _():
            here = slice(slot * ROWS, (slot + 1) * ROWS)
            target[:, here] = source[here, :].T


def softmax_steps(sc, starts, q, tiles, kc, vt, top, total, acc, j):
    row0 = pl.multiple_of(j * UNIT, UNIT)
    q_unit = stacked(q, row0)
    start, row = starts[pl.ds(j, 1), :], unit_rows(j)
    one = pl.ds(j, 1)
    mine = pl.ds(pl.multiple_of(j * HEAD, HEAD), HEAD)

    def block(first_key, needs_mask):
        here = pl.ds(pl.multiple_of(first_key - tiles[0] * ROWS, KEYS), KEYS)
        s = dot(kc[here, :], q_unit, NT) * SCALE_LOG2
        if needs_mask:
            s = masked(s, first_key, start, row)
        old = top[one, :]
        new = jnp.maximum(old, jnp.max(s, axis=0, keepdims=True))
        p = jnp.exp2(s - new)
        shrink = jnp.exp2(old - new)
        top[one, :] = new
        total[one, :] = total[one, :] * shrink + jnp.sum(p, axis=0, keepdims=True)
        acc[mine, :] = acc[mine, :] * shrink + dot(vt[:, here], p.astype(jnp.bfloat16))

    over_keys(sc, j, tiles, KEYS, block)


NEAR_TILES = tuple(range(FAR, REACH + 1))
FAR_TILES = tuple(range(FAR))
BEFORE_TILES = tuple(range(REACH))
OWN_TILES = (REACH,)


def forward_near(sc, starts, q_all, *refs):
    nears, (top, total, acc, kc, vc, vt, q, sems) = refs[:4], refs[4:]
    top[...] = jnp.full(top.shape, NEG_BIG, jnp.float32)
    fetch(near_pieces(sc[0], *nears), kc, vc, [(q_all, q)], sems, lambda: clear(total, acc))
    transposed(sc, NEAR_TILES, vc, vt)

    @pl.loop(0, UNITS)
    def _(j):
        softmax_steps(sc, starts, q, NEAR_TILES, kc, vt, top, total, acc, j)


def forward_far(sc, starts, top0, total0, acc0, q_all, g_all, w_all, *refs):
    fars, (attn, norm, delta, left, right, kc, vc, vt, q, g, w, top, total, acc, sems) = refs[:3], refs[3:]
    weight = pltpu.make_async_copy(w_all, w, sems.at[13])
    weight.start()
    par, y, zl = sc[0], sc[1], sc[2]

    def meanwhile():
        top[...] = top0[...]
        total[...] = total0[...]
        acc[...] = acc0[...]

    fetch(far_pieces(par, *fars), kc, vc, [(q_all, q), (g_all, g)], sems, meanwhile)
    transposed(sc, FAR_TILES, vc, vt)

    @pl.loop(0, UNITS)
    def _(j):
        softmax_steps(sc, starts, q, FAR_TILES, kc, vt, top, total, acc, j)
        one = pl.ds(j, 1)
        out = acc[pl.ds(pl.multiple_of(j * HEAD, HEAD), HEAD), :] / total[one, :]
        norm[one, :] = top[one, :] + jnp.log2(total[one, :])
        g_unit = stacked(g, pl.multiple_of(j * UNIT, UNIT)).astype(jnp.float32).T
        delta[one, :] = jnp.sum(out * g_unit, axis=0, keepdims=True)
        flat = out.T.astype(jnp.bfloat16)
        for part in range(UNIT // BLOCK):
            number = j * (UNIT // BLOCK) + part
            place = 2 * ((number - y) & 3) + ((number >> 2) ^ zl)
            rows = pl.ds(pl.multiple_of(place * BLOCK, BLOCK), BLOCK)
            for h in range(HEADS_DEV):
                first = h * UNIT + part * BLOCK
                attn[rows, h * HEAD : (h + 1) * HEAD] = flat[first : first + BLOCK]

    weight.wait()
    cut = w.shape[1] // 2
    opposite = attn[4 * BLOCK : 6 * BLOCK, :]
    left[...] = dot(opposite, w[:, :cut]).astype(jnp.bfloat16)
    right[...] = dot(opposite, w[:, cut:]).astype(jnp.bfloat16)


def add_arrived(after, before, from_left, from_right, after_out, after_mine, before_out, before_mine):
    cut = from_left.shape[1]
    for rows, after_to, before_to in (
        (slice(0, BLOCK), after_mine, before_mine),
        (slice(BLOCK, 2 * BLOCK), after_out, before_out),
    ):
        there = after[rows, :cut].astype(jnp.float32) + from_left[rows, :].astype(jnp.float32)
        back = before[rows, cut:].astype(jnp.float32) + from_right[rows, :].astype(jnp.float32)
        after_to[:, :cut] = there.astype(jnp.bfloat16)
        after_to[:, cut:] = after[rows, cut:]
        before_to[:, :cut] = before[rows, :cut]
        before_to[:, cut:] = back.astype(jnp.bfloat16)


def gradient_steps(sc, starts, norm, delta, q, g, tiles, keys, kc, vc, kt, dk, dv, dq, j):
    row0 = pl.multiple_of(j * UNIT, UNIT)
    q_unit, g_unit = stacked(q, row0), stacked(g, row0)
    start, row = starts[pl.ds(j, 1), :], unit_rows(j)
    norm_unit, delta_unit = norm[pl.ds(j, 1), :], delta[pl.ds(j, 1), :]
    mine = pl.ds(pl.multiple_of(j * HEAD, HEAD), HEAD)

    def block(first_key, needs_mask):
        here = pl.ds(pl.multiple_of(first_key - tiles[0] * ROWS, keys), keys)
        s = dot(kc[here, :], q_unit, NT) * SCALE_LOG2
        if needs_mask:
            s = masked(s, first_key, start, row)
        p = jnp.exp2(s - norm_unit)
        dp = dot(vc[here, :], g_unit, NT)
        ds = (p * (dp - delta_unit)).astype(jnp.bfloat16)
        dk[here, :] += dot(ds, q_unit)
        dv[here, :] += dot(p.astype(jnp.bfloat16), g_unit)
        dq[mine, :] += dot(kt[:, here], ds)

    over_keys(sc, j, tiles, keys, block)


def tile_out(ref, dk, dv, slot):
    here = slice(slot * ROWS, (slot + 1) * ROWS)
    ref[0] = (dk[here, :] * SCALE).astype(jnp.bfloat16)
    ref[1] = dv[here, :].astype(jnp.bfloat16)


def clear(*refs):
    for ref in refs:
        ref[...] = jnp.zeros(ref.shape, jnp.float32)


def backward_before(sc, starts, norm, delta, attn, q_all, g_all, w_all, *refs):
    tiles, (dq, first, third, given, here, other, after, before, kc, vc, kt, q, g, w, dk, dv, sems) = refs[:5], refs[5:]
    weight = pltpu.make_async_copy(w_all, w, sems.at[13])
    weight.start()
    fetch(before_pieces(sc[0], *tiles), kc, vc, [(q_all, q), (g_all, g)], sems, lambda: clear(dq, dk, dv))
    transposed(sc, BEFORE_TILES, kc, kt)

    @pl.loop(0, UNITS)
    def _(j):
        gradient_steps(sc, starts, norm, delta, q, g, BEFORE_TILES, KEYS, kc, vc, kt, dk, dv, dq, j)

    tile_out(first, dk, dv, 0)
    tile_out(given.at[:2], dk, dv, 1)
    tile_out(third, dk, dv, 2)
    tile_out(given.at[2:], dk, dv, 3)
    weight.wait()
    for first_column in range(0, w.shape[1], 1024):
        part = slice(first_column, first_column + 1024)
        product = dot(attn[: 4 * BLOCK, :], w[:, part]).astype(jnp.bfloat16)
        here[:, part] = product[:BLOCK]
        other[:, part] = product[BLOCK : 2 * BLOCK]
        after[:, part] = product[2 * BLOCK :]
        before[:, part] = dot(attn[6 * BLOCK :, :], w[:, part]).astype(jnp.bfloat16)


def backward_own(sc, starts, norm, delta, dq0, q_all, g_all, own, gq, last, kc, vc, kt, q, g, dk, dv, dq, sems):
    def meanwhile():
        clear(dk, dv)
        dq[...] = dq0[...]

    fetch([(own, 0)], kc, vc, [(q_all, q), (g_all, g)], sems, meanwhile)
    transposed(sc, OWN_TILES, kc, kt)

    @pl.loop(0, UNITS)
    def _(j):
        gradient_steps(sc, starts, norm, delta, q, g, OWN_TILES, UNIT, kc, vc, kt, dk, dv, dq, j)
        flat = (dq[pl.ds(pl.multiple_of(j * HEAD, HEAD), HEAD), :] * SCALE).T.astype(jnp.bfloat16)
        row0 = pl.multiple_of(j * UNIT, UNIT)
        for h in range(HEADS_DEV):
            gq[pl.ds(row0, UNIT), h * HEAD : (h + 1) * HEAD] = flat[h * UNIT : (h + 1) * UNIT]

    tile_out(last, dk, dv, 0)


def pack(k, v, both):
    both[0] = k[...]
    both[1] = v[...]


VMEM = pl.BlockSpec(memory_space=pltpu.VMEM)
SMEM = pl.BlockSpec(memory_space=pltpu.SMEM)
ANY = pl.BlockSpec(memory_space=pl.ANY)
COST = pl.CostEstimate(flops=10**6, bytes_accessed=2**10, transcendentals=0)
TILE = (2, ROWS, HEAD)
STAT = (UNITS, COLS)
SUMS = (UNITS * HEAD, COLS)


def f32(shape):
    return jax.ShapeDtypeStruct(shape, jnp.float32)


def bf16(shape):
    return jax.ShapeDtypeStruct(shape, jnp.bfloat16)


def call(kernel, outs, dense, whole, tiles, scratch, slots):
    keys = pltpu.VMEM((slots * ROWS, HEAD), jnp.bfloat16)
    return pl.pallas_call(
        kernel,
        out_shape=outs,
        in_specs=[SMEM] + [VMEM] * (len(dense) - 1) + [ANY] * (len(whole) + len(tiles)),
        out_specs=[VMEM] * len(outs),
        scratch_shapes=[keys, keys, pltpu.VMEM((HEAD, (slots - 1) * ROWS), jnp.bfloat16)]
        + [pltpu.VMEM(array.shape, array.dtype) for array in whole]
        + [pltpu.VMEM(shape, jnp.float32) for shape in scratch]
        + [pltpu.SemaphoreType.DMA((14,))],
        compiler_params=pltpu.CompilerParams(vmem_limit_bytes=60 * 2**20),
        cost_estimate=COST,
        name=kernel.__name__,
    )(*dense, *whole, *tiles)


def shifted(x, distance):
    n = lax.axis_size("dp")
    return lax.ppermute(x, "dp", [(i, i + distance) for i in range(n) if 0 <= i + distance < n])


def twinned(x):
    return lax.ppermute(x, "dp", [(i, i ^ 1) for i in range(lax.axis_size("dp"))])


def along_y(x, step):
    return lax.ppermute(x, "tensor", [(i, (i & 4) | ((i + step) & 3)) for i in range(8)])


def across_z(x):
    return lax.ppermute(x, "tensor", [(i, i ^ 4) for i in range(8)])


def half(x):
    return x.astype(jnp.bfloat16)


def wide(x):
    return x.astype(jnp.float32)


def on_device(queries, key_rows, value_rows, grad_out, out_weight, lengths):
    dp, tensor = lax.axis_index("dp"), lax.axis_index("tensor")
    par = dp & 1
    odd = par == 1
    own = pl.pallas_call(pack, out_shape=bf16(TILE), name="pack")(key_rows, value_rows)
    near = shifted(own, 2)
    twin_own = twinned(own)
    far = shifted(own, 4)
    near_twin = twinned(near)

    base = (dp - REACH) * ROWS
    position = dp * ROWS + jnp.arange(ROWS, dtype=jnp.int32)
    ends = jnp.cumsum(lengths)
    start = jnp.max(jnp.where(ends[None, :] <= position[:, None], ends[None, :], 0), axis=1) - base
    start = start.reshape(UNITS, UNIT)
    head = jnp.stack([par, tensor & 3, tensor >> 2])
    sc = jnp.concatenate([head, start[:, 0], start[:, -1]]).astype(jnp.int32)
    starts = jnp.tile(start, (1, HEADS_DEV)).astype(jnp.int32)

    nears = (own, near, twin_own, near_twin)
    state = call(forward_near, (f32(STAT), f32(STAT), f32(SUMS)), (sc, starts), (queries,), nears, (), 4)
    far, state = lax.optimization_barrier((far, state))
    fars = (far, twinned(far), near_twin)
    sent = bf16((2 * BLOCK, out_weight.shape[1] // 2))
    attn, norm, delta, left, right = call(
        forward_far,
        (bf16(queries.shape), f32(STAT), f32(STAT), sent, sent),
        (sc, starts, *state),
        (queries, grad_out, out_weight),
        fars,
        (STAT, STAT, SUMS),
        3,
    )
    from_left, from_right = along_y(left, 1), along_y(right, -1)

    asked, whole = (sc, starts, norm, delta), (queries, grad_out)
    keys = (REACH * ROWS, HEAD)
    single, double = (bf16((n * BLOCK, out_weight.shape[1])) for n in (1, 2))
    dq, first, third, given, here, other, after, before = call(
        backward_before,
        (f32(SUMS), bf16(TILE), bf16(TILE), bf16((4, ROWS, HEAD)), single, single, double, double),
        (*asked, attn),
        (*whole, out_weight),
        (near, twin_own, near_twin, far, fars[1]),
        (keys, keys),
        REACH + 1,
    )
    from_left, from_right, dq, first, third, given, after, before = lax.optimization_barrier(
        (from_left, from_right, dq, first, third, given, after, before)
    )

    got = twinned(given)
    after, after_mine, before, before_mine = pl.pallas_call(
        add_arrived, out_shape=[single] * 4, cost_estimate=COST, name="add_arrived"
    )(after, before, from_left, from_right)
    from_left, from_right = along_y(after, 1), along_y(before, -1)
    far_sum = half(wide(first) + jnp.where(odd, wide(got[:2]), 0.0))
    near_sum = half(wide(third) + jnp.where(odd, wide(got[2:]), wide(got[:2])))
    far_sum, near_sum, dq = lax.optimization_barrier((far_sum, near_sum, dq))
    far_sum, near_sum = shifted(far_sum, -4), shifted(near_sum, -2)
    keys = (ROWS, HEAD)
    gq, last = call(
        backward_own, (bf16(queries.shape), bf16(TILE)), (*asked, dq), whole, (own,), (keys, keys, SUMS), 2
    )
    from_left, from_right, after_mine, before_mine, far_sum, near_sum, gq, last = lax.optimization_barrier(
        (from_left, from_right, after_mine, before_mine, far_sum, near_sum, gq, last)
    )
    other = half(wide(other) + wide(from_left) + wide(from_right))
    other, after_mine, before_mine = lax.optimization_barrier((other, after_mine, before_mine))
    from_left, from_right = along_y(after_mine, 1), along_y(before_mine, -1)
    other = across_z(other)
    own_sum = half(wide(last) + jnp.where(odd, 0.0, wide(got[2:])) + wide(near_sum) + wide(far_sum))
    projected = half(wide(here) + wide(from_left) + wide(from_right) + wide(other))
    return projected, gq, own_sum[0], own_sum[1]


def solution(mesh):
    split = P("dp", "tensor")
    return jax.shard_map(
        on_device,
        mesh=mesh,
        in_specs=(split, split, split, split, P("tensor", None), P()),
        out_specs=(P(("dp", "tensor"), None), split, split, split),
        check_vma=False,
    )
```

```python
import jax
import jax.numpy as jnp
from jax import lax
from jax.experimental import pallas as pl
from jax.experimental.pallas import tpu as pltpu
from jax.sharding import PartitionSpec as P

HEAD = 128
HEADS_DEV = 4
REACH = 4
FAR = 2
ROWS = 512
BLOCK = 64
UNIT = 256
COLS = UNIT * HEADS_DEV
UNITS = ROWS // UNIT
KEYS = 512
NEG_BIG = -1e30
SCALE = HEAD**-0.5
NT = (((1,), (1,)), ((), ()))
NN = (((1,), (0,)), ((), ()))


def dot(a, b, dims=NN):
    return lax.dot_general(a, b, dims, preferred_element_type=jnp.float32)


def fetch(pieces, kc, vc, whole, sems, meanwhile=lambda: None):
    copies = [pltpu.make_async_copy(*pair, sems.at[10 + i]) for i, pair in enumerate(whole)]
    for number, (tile, slot) in enumerate(pieces):
        first = slot * ROWS
        here = pl.ds(first if isinstance(first, int) else pl.multiple_of(first, ROWS), ROWS)
        copies.append(pltpu.make_async_copy(tile.at[0], kc.at[here], sems.at[2 * number]))
        copies.append(pltpu.make_async_copy(tile.at[1], vc.at[here], sems.at[2 * number + 1]))
    for copy in copies:
        copy.start()
    meanwhile()
    for copy in copies:
        copy.wait()


def near_pieces(par, own, near, twin_own, near_twin):
    return [(near, 0), (own, 2), (twin_own, 3 - 2 * par), (near_twin, 1 + 2 * par)]


def before_pieces(par, near, twin_own, near_twin, far, far_twin):
    return [(far, 0), (near, 2), (near_twin, 3 - 2 * par), (far_twin, 1 + 3 * par), (twin_own, 4 - par)]


def far_pieces(par, far, far_twin, near_twin):
    return [(far, 0), (far_twin, 1 + par), (near_twin, 2 - par)]


def stacked(ref, row0):
    return jnp.concatenate(
        [ref[pl.ds(row0, UNIT), h * HEAD : (h + 1) * HEAD] for h in range(HEADS_DEV)], axis=0
    )


def masked(scores, first_key, start, row):
    key = first_key + lax.broadcasted_iota(jnp.int32, scores.shape, 0)
    return jnp.where((key >= start) & (key <= row), scores, NEG_BIG)


def unit_rows(j):
    lane = lax.broadcasted_iota(jnp.int32, (1, COLS), 1)
    return REACH * ROWS + j * UNIT + (lane & (UNIT - 1))


def over_keys(sc, j, tiles, keys, block):
    lowest, highest = sc[3 + j], sc[3 + UNITS + j]
    first_row = REACH * ROWS + j * UNIT
    begin = jnp.maximum(lowest, tiles[0] * ROWS) // keys
    end = jnp.minimum((first_row + UNIT - 1) // keys + 1, (tiles[-1] + 1) * ROWS // keys)

    @pl.loop(begin, end)
    def _(kb):
        first_key = pl.multiple_of(kb * keys, keys)
        whole = (first_key >= highest) & (first_key + keys - 1 <= first_row)

        @pl.when(whole)
        def _():
            block(first_key, False)

        @pl.when(jnp.logical_not(whole))
        def _():
            block(first_key, True)


def transposed(sc, tiles, source, target):
    for slot, tile in enumerate(tiles):

        @pl.when((tile + 1) * ROWS > sc[3])
        def _():
            here = slice(slot * ROWS, (slot + 1) * ROWS)
            target[:, here] = source[here, :].T


def softmax_steps(sc, starts, q, tiles, kc, vt, top, total, acc, j):
    row0 = pl.multiple_of(j * UNIT, UNIT)
    q_unit = stacked(q, row0)
    start, row = starts[pl.ds(j, 1), :], unit_rows(j)
    one = pl.ds(j, 1)
    mine = pl.ds(pl.multiple_of(j * HEAD, HEAD), HEAD)

    def block(first_key, needs_mask):
        here = pl.ds(pl.multiple_of(first_key - tiles[0] * ROWS, KEYS), KEYS)
        s = dot(kc[here, :], q_unit, NT) * SCALE
        if needs_mask:
            s = masked(s, first_key, start, row)
        old = top[one, :]
        new = jnp.maximum(old, jnp.max(s, axis=0, keepdims=True))
        p = jnp.exp(s - new)
        shrink = jnp.exp(old - new)
        top[one, :] = new
        total[one, :] = total[one, :] * shrink + jnp.sum(p, axis=0, keepdims=True)
        acc[mine, :] = acc[mine, :] * shrink + dot(vt[:, here], p.astype(jnp.bfloat16))

    over_keys(sc, j, tiles, KEYS, block)


NEAR_TILES = tuple(range(FAR, REACH + 1))
FAR_TILES = tuple(range(FAR))
BEFORE_TILES = tuple(range(REACH))
OWN_TILES = (REACH,)


def forward_near(sc, starts, q_all, *refs):
    nears, (top, total, acc, kc, vc, vt, q, sems) = refs[:4], refs[4:]
    top[...] = jnp.full(top.shape, NEG_BIG, jnp.float32)
    fetch(near_pieces(sc[0], *nears), kc, vc, [(q_all, q)], sems, lambda: clear(total, acc))
    transposed(sc, NEAR_TILES, vc, vt)

    @pl.loop(0, UNITS)
    def _(j):
        softmax_steps(sc, starts, q, NEAR_TILES, kc, vt, top, total, acc, j)


def forward_far(sc, starts, top0, total0, acc0, q_all, g_all, w_all, *refs):
    fars, (attn, norm, delta, left, right, kc, vc, vt, q, g, w, top, total, acc, sems) = refs[:3], refs[3:]
    weight = pltpu.make_async_copy(w_all, w, sems.at[13])
    weight.start()
    par, y, zl = sc[0], sc[1], sc[2]

    def meanwhile():
        top[...] = top0[...]
        total[...] = total0[...]
        acc[...] = acc0[...]

    fetch(far_pieces(par, *fars), kc, vc, [(q_all, q), (g_all, g)], sems, meanwhile)
    transposed(sc, FAR_TILES, vc, vt)

    @pl.loop(0, UNITS)
    def _(j):
        softmax_steps(sc, starts, q, FAR_TILES, kc, vt, top, total, acc, j)
        one = pl.ds(j, 1)
        out = acc[pl.ds(pl.multiple_of(j * HEAD, HEAD), HEAD), :] / total[one, :]
        norm[one, :] = top[one, :] + jnp.log(total[one, :])
        g_unit = stacked(g, pl.multiple_of(j * UNIT, UNIT)).astype(jnp.float32).T
        delta[one, :] = jnp.sum(out * g_unit, axis=0, keepdims=True)
        flat = out.T.astype(jnp.bfloat16)
        for part in range(UNIT // BLOCK):
            number = j * (UNIT // BLOCK) + part
            place = 2 * ((number - y) & 3) + ((number >> 2) ^ zl)
            rows = pl.ds(pl.multiple_of(place * BLOCK, BLOCK), BLOCK)
            for h in range(HEADS_DEV):
                first = h * UNIT + part * BLOCK
                attn[rows, h * HEAD : (h + 1) * HEAD] = flat[first : first + BLOCK]

    weight.wait()
    cut = w.shape[1] // 2
    opposite = attn[4 * BLOCK : 6 * BLOCK, :]
    left[...] = dot(opposite, w[:, :cut]).astype(jnp.bfloat16)
    right[...] = dot(opposite, w[:, cut:]).astype(jnp.bfloat16)


def add_arrived(after, before, from_left, from_right, after_out, after_mine, before_out, before_mine):
    cut = from_left.shape[1]
    for rows, after_to, before_to in (
        (slice(0, BLOCK), after_mine, before_mine),
        (slice(BLOCK, 2 * BLOCK), after_out, before_out),
    ):
        there = after[rows, :cut].astype(jnp.float32) + from_left[rows, :].astype(jnp.float32)
        back = before[rows, cut:].astype(jnp.float32) + from_right[rows, :].astype(jnp.float32)
        after_to[:, :cut] = there.astype(jnp.bfloat16)
        after_to[:, cut:] = after[rows, cut:]
        before_to[:, :cut] = before[rows, :cut]
        before_to[:, cut:] = back.astype(jnp.bfloat16)


def gradient_steps(sc, starts, norm, delta, q, g, tiles, keys, kc, vc, kt, dk, dv, dq, j):
    row0 = pl.multiple_of(j * UNIT, UNIT)
    q_unit, g_unit = stacked(q, row0), stacked(g, row0)
    start, row = starts[pl.ds(j, 1), :], unit_rows(j)
    norm_unit, delta_unit = norm[pl.ds(j, 1), :], delta[pl.ds(j, 1), :]
    mine = pl.ds(pl.multiple_of(j * HEAD, HEAD), HEAD)

    def block(first_key, needs_mask):
        here = pl.ds(pl.multiple_of(first_key - tiles[0] * ROWS, keys), keys)
        s = dot(kc[here, :], q_unit, NT) * SCALE
        if needs_mask:
            s = masked(s, first_key, start, row)
        p = jnp.exp(s - norm_unit)
        dp = dot(vc[here, :], g_unit, NT)
        ds = (p * (dp - delta_unit)).astype(jnp.bfloat16)
        dk[here, :] += dot(ds, q_unit)
        dv[here, :] += dot(p.astype(jnp.bfloat16), g_unit)
        dq[mine, :] += dot(kt[:, here], ds)

    over_keys(sc, j, tiles, keys, block)


def tile_out(ref, dk, dv, slot):
    here = slice(slot * ROWS, (slot + 1) * ROWS)
    ref[0] = (dk[here, :] * SCALE).astype(jnp.bfloat16)
    ref[1] = dv[here, :].astype(jnp.bfloat16)


def clear(*refs):
    for ref in refs:
        ref[...] = jnp.zeros(ref.shape, jnp.float32)


def backward_before(sc, starts, norm, delta, attn, q_all, g_all, w_all, *refs):
    tiles, (dq, first, third, given, here, other, after, before, kc, vc, kt, q, g, w, dk, dv, sems) = refs[:5], refs[5:]
    weight = pltpu.make_async_copy(w_all, w, sems.at[13])
    weight.start()
    fetch(before_pieces(sc[0], *tiles), kc, vc, [(q_all, q), (g_all, g)], sems, lambda: clear(dq, dk, dv))
    transposed(sc, BEFORE_TILES, kc, kt)

    @pl.loop(0, UNITS)
    def _(j):
        gradient_steps(sc, starts, norm, delta, q, g, BEFORE_TILES, KEYS, kc, vc, kt, dk, dv, dq, j)

    tile_out(first, dk, dv, 0)
    tile_out(given.at[:2], dk, dv, 1)
    tile_out(third, dk, dv, 2)
    tile_out(given.at[2:], dk, dv, 3)
    weight.wait()
    for first_column in range(0, w.shape[1], 1024):
        part = slice(first_column, first_column + 1024)
        product = dot(attn[: 4 * BLOCK, :], w[:, part]).astype(jnp.bfloat16)
        here[:, part] = product[:BLOCK]
        other[:, part] = product[BLOCK : 2 * BLOCK]
        after[:, part] = product[2 * BLOCK :]
        before[:, part] = dot(attn[6 * BLOCK :, :], w[:, part]).astype(jnp.bfloat16)


def backward_own(sc, starts, norm, delta, dq0, q_all, g_all, own, gq, last, kc, vc, kt, q, g, dk, dv, dq, sems):
    def meanwhile():
        clear(dk, dv)
        dq[...] = dq0[...]

    fetch([(own, 0)], kc, vc, [(q_all, q), (g_all, g)], sems, meanwhile)
    transposed(sc, OWN_TILES, kc, kt)

    @pl.loop(0, UNITS)
    def _(j):
        gradient_steps(sc, starts, norm, delta, q, g, OWN_TILES, UNIT, kc, vc, kt, dk, dv, dq, j)
        flat = (dq[pl.ds(pl.multiple_of(j * HEAD, HEAD), HEAD), :] * SCALE).T.astype(jnp.bfloat16)
        row0 = pl.multiple_of(j * UNIT, UNIT)
        for h in range(HEADS_DEV):
            gq[pl.ds(row0, UNIT), h * HEAD : (h + 1) * HEAD] = flat[h * UNIT : (h + 1) * UNIT]

    tile_out(last, dk, dv, 0)


def pack(k, v, both):
    both[0] = k[...]
    both[1] = v[...]


VMEM = pl.BlockSpec(memory_space=pltpu.VMEM)
SMEM = pl.BlockSpec(memory_space=pltpu.SMEM)
ANY = pl.BlockSpec(memory_space=pl.ANY)
COST = pl.CostEstimate(flops=10**6, bytes_accessed=2**10, transcendentals=0)
TILE = (2, ROWS, HEAD)
STAT = (UNITS, COLS)
SUMS = (UNITS * HEAD, COLS)


def f32(shape):
    return jax.ShapeDtypeStruct(shape, jnp.float32)


def bf16(shape):
    return jax.ShapeDtypeStruct(shape, jnp.bfloat16)


def call(kernel, outs, dense, whole, tiles, scratch, slots):
    keys = pltpu.VMEM((slots * ROWS, HEAD), jnp.bfloat16)
    return pl.pallas_call(
        kernel,
        out_shape=outs,
        in_specs=[SMEM] + [VMEM] * (len(dense) - 1) + [ANY] * (len(whole) + len(tiles)),
        out_specs=[VMEM] * len(outs),
        scratch_shapes=[keys, keys, pltpu.VMEM((HEAD, (slots - 1) * ROWS), jnp.bfloat16)]
        + [pltpu.VMEM(array.shape, array.dtype) for array in whole]
        + [pltpu.VMEM(shape, jnp.float32) for shape in scratch]
        + [pltpu.SemaphoreType.DMA((14,))],
        compiler_params=pltpu.CompilerParams(vmem_limit_bytes=60 * 2**20),
        cost_estimate=COST,
        name=kernel.__name__,
    )(*dense, *whole, *tiles)


def shifted(x, distance):
    n = lax.axis_size("dp")
    return lax.ppermute(x, "dp", [(i, i + distance) for i in range(n) if 0 <= i + distance < n])


def twinned(x):
    return lax.ppermute(x, "dp", [(i, i ^ 1) for i in range(lax.axis_size("dp"))])


def along_y(x, step):
    return lax.ppermute(x, "tensor", [(i, (i & 4) | ((i + step) & 3)) for i in range(8)])


def across_z(x):
    return lax.ppermute(x, "tensor", [(i, i ^ 4) for i in range(8)])


def half(x):
    return x.astype(jnp.bfloat16)


def wide(x):
    return x.astype(jnp.float32)


def on_device(queries, key_rows, value_rows, grad_out, out_weight, lengths):
    dp, tensor = lax.axis_index("dp"), lax.axis_index("tensor")
    par = dp & 1
    odd = par == 1
    own = pl.pallas_call(pack, out_shape=bf16(TILE), name="pack")(key_rows, value_rows)
    near = shifted(own, 2)
    twin_own = twinned(own)
    far = shifted(own, 4)
    near_twin = twinned(near)

    base = (dp - REACH) * ROWS
    position = dp * ROWS + jnp.arange(ROWS, dtype=jnp.int32)
    ends = jnp.cumsum(lengths)
    start = jnp.max(jnp.where(ends[None, :] <= position[:, None], ends[None, :], 0), axis=1) - base
    start = start.reshape(UNITS, UNIT)
    head = jnp.stack([par, tensor & 3, tensor >> 2])
    sc = jnp.concatenate([head, start[:, 0], start[:, -1]]).astype(jnp.int32)
    starts = jnp.tile(start, (1, HEADS_DEV)).astype(jnp.int32)

    nears = (own, near, twin_own, near_twin)
    state = call(forward_near, (f32(STAT), f32(STAT), f32(SUMS)), (sc, starts), (queries,), nears, (), 4)
    far, state = lax.optimization_barrier((far, state))
    fars = (far, twinned(far), near_twin)
    sent = bf16((2 * BLOCK, out_weight.shape[1] // 2))
    attn, norm, delta, left, right = call(
        forward_far,
        (bf16(queries.shape), f32(STAT), f32(STAT), sent, sent),
        (sc, starts, *state),
        (queries, grad_out, out_weight),
        fars,
        (STAT, STAT, SUMS),
        3,
    )
    from_left, from_right = along_y(left, 1), along_y(right, -1)

    asked, whole = (sc, starts, norm, delta), (queries, grad_out)
    keys = (REACH * ROWS, HEAD)
    single, double = (bf16((n * BLOCK, out_weight.shape[1])) for n in (1, 2))
    dq, first, third, given, here, other, after, before = call(
        backward_before,
        (f32(SUMS), bf16(TILE), bf16(TILE), bf16((4, ROWS, HEAD)), single, single, double, double),
        (*asked, attn),
        (*whole, out_weight),
        (near, twin_own, near_twin, far, fars[1]),
        (keys, keys),
        REACH + 1,
    )
    from_left, from_right, dq, first, third, given, after, before = lax.optimization_barrier(
        (from_left, from_right, dq, first, third, given, after, before)
    )

    got = twinned(given)
    after, after_mine, before, before_mine = pl.pallas_call(
        add_arrived, out_shape=[single] * 4, cost_estimate=COST, name="add_arrived"
    )(after, before, from_left, from_right)
    from_left, from_right = along_y(after, 1), along_y(before, -1)
    far_sum = half(wide(first) + jnp.where(odd, wide(got[:2]), 0.0))
    near_sum = half(wide(third) + jnp.where(odd, wide(got[2:]), wide(got[:2])))
    far_sum, near_sum, dq = lax.optimization_barrier((far_sum, near_sum, dq))
    far_sum, near_sum = shifted(far_sum, -4), shifted(near_sum, -2)
    keys = (ROWS, HEAD)
    gq, last = call(
        backward_own, (bf16(queries.shape), bf16(TILE)), (*asked, dq), whole, (own,), (keys, keys, SUMS), 2
    )
    from_left, from_right, after_mine, before_mine, far_sum, near_sum, gq, last = lax.optimization_barrier(
        (from_left, from_right, after_mine, before_mine, far_sum, near_sum, gq, last)
    )
    other = half(wide(other) + wide(from_left) + wide(from_right))
    other, after_mine, before_mine = lax.optimization_barrier((other, after_mine, before_mine))
    from_left, from_right = along_y(after_mine, 1), along_y(before_mine, -1)
    other = across_z(other)
    own_sum = half(wide(last) + jnp.where(odd, 0.0, wide(got[2:])) + wide(near_sum) + wide(far_sum))
    projected = half(wide(here) + wide(from_left) + wide(from_right) + wide(other))
    return projected, gq, own_sum[0], own_sum[1]


def solution(mesh):
    split = P("dp", "tensor")
    return jax.shard_map(
        on_device,
        mesh=mesh,
        in_specs=(split, split, split, split, P("tensor", None), P()),
        out_specs=(P(("dp", "tensor"), None), split, split, split),
        check_vma=False,
    )
```

```python
import math

import jax
import jax.numpy as jnp
from jax import lax
from jax.experimental import pallas as pl
from jax.experimental.pallas import tpu as pltpu
from jax.sharding import PartitionSpec as P

HEAD = 128
HEADS_DEV = 4
REACH = 4
FAR = 2
ROWS = 512
BLOCK = 64
UNIT = 512
COLS = UNIT * HEADS_DEV
UNITS = ROWS // UNIT
KEYS = 512
NEG_BIG = -1e30
SCALE = HEAD**-0.5
SCALE_LOG2 = SCALE * math.log2(math.e)
NT = (((1,), (1,)), ((), ()))
NN = (((1,), (0,)), ((), ()))


def dot(a, b, dims=NN):
    return lax.dot_general(a, b, dims, preferred_element_type=jnp.float32)


def fetch(pieces, kc, vc, whole, sems, meanwhile=lambda: None):
    copies = [pltpu.make_async_copy(*pair, sems.at[10 + i]) for i, pair in enumerate(whole)]
    for number, (tile, slot) in enumerate(pieces):
        first = slot * ROWS
        here = pl.ds(first if isinstance(first, int) else pl.multiple_of(first, ROWS), ROWS)
        copies.append(pltpu.make_async_copy(tile.at[0], kc.at[here], sems.at[2 * number]))
        copies.append(pltpu.make_async_copy(tile.at[1], vc.at[here], sems.at[2 * number + 1]))
    for copy in copies:
        copy.start()
    meanwhile()
    for copy in copies:
        copy.wait()


def near_pieces(par, own, near, twin_own, near_twin):
    return [(near, 0), (own, 2), (twin_own, 3 - 2 * par), (near_twin, 1 + 2 * par)]


def before_pieces(par, near, twin_own, near_twin, far, far_twin):
    return [(far, 0), (near, 2), (near_twin, 3 - 2 * par), (far_twin, 1 + 3 * par), (twin_own, 4 - par)]


def far_pieces(par, far, far_twin, near_twin):
    return [(far, 0), (far_twin, 1 + par), (near_twin, 2 - par)]


def stacked(ref, row0):
    return jnp.concatenate(
        [ref[pl.ds(row0, UNIT), h * HEAD : (h + 1) * HEAD] for h in range(HEADS_DEV)], axis=0
    )


def masked(scores, first_key, start, row):
    key = first_key + lax.broadcasted_iota(jnp.int32, scores.shape, 0)
    return jnp.where((key >= start) & (key <= row), scores, NEG_BIG)


def unit_rows(j):
    lane = lax.broadcasted_iota(jnp.int32, (1, COLS), 1)
    return REACH * ROWS + j * UNIT + (lane & (UNIT - 1))


def over_keys(sc, j, tiles, keys, block):
    lowest, highest = sc[3 + j], sc[3 + UNITS + j]
    first_row = REACH * ROWS + j * UNIT
    begin = jnp.maximum(lowest, tiles[0] * ROWS) // keys
    end = jnp.minimum((first_row + UNIT - 1) // keys + 1, (tiles[-1] + 1) * ROWS // keys)

    @pl.loop(begin, end)
    def _(kb):
        first_key = pl.multiple_of(kb * keys, keys)
        whole = (first_key >= highest) & (first_key + keys - 1 <= first_row)

        @pl.when(whole)
        def _():
            block(first_key, False)

        @pl.when(jnp.logical_not(whole))
        def _():
            block(first_key, True)


def transposed(sc, tiles, source, target):
    for slot, tile in enumerate(tiles):

        @pl.when((tile + 1) * ROWS > sc[3])
        def _():
            here = slice(slot * ROWS, (slot + 1) * ROWS)
            target[:, here] = source[here, :].T


def softmax_steps(sc, starts, q, tiles, kc, vt, top, total, acc, j):
    row0 = pl.multiple_of(j * UNIT, UNIT)
    q_unit = stacked(q, row0)
    start, row = starts[pl.ds(j, 1), :], unit_rows(j)
    one = pl.ds(j, 1)
    mine = pl.ds(pl.multiple_of(j * HEAD, HEAD), HEAD)

    def block(first_key, needs_mask):
        here = pl.ds(pl.multiple_of(first_key - tiles[0] * ROWS, KEYS), KEYS)
        s = dot(kc[here, :], q_unit, NT) * SCALE_LOG2
        if needs_mask:
            s = masked(s, first_key, start, row)
        old = top[one, :]
        new = jnp.maximum(old, jnp.max(s, axis=0, keepdims=True))
        p = jnp.exp2(s - new)
        shrink = jnp.exp2(old - new)
        top[one, :] = new
        total[one, :] = total[one, :] * shrink + jnp.sum(p, axis=0, keepdims=True)
        acc[mine, :] = acc[mine, :] * shrink + dot(vt[:, here], p.astype(jnp.bfloat16))

    over_keys(sc, j, tiles, KEYS, block)


NEAR_TILES = tuple(range(FAR, REACH + 1))
FAR_TILES = tuple(range(FAR))
BEFORE_TILES = tuple(range(REACH))
OWN_TILES = (REACH,)


def forward_near(sc, starts, q_all, *refs):
    nears, (top, total, acc, kc, vc, vt, q, sems) = refs[:4], refs[4:]
    top[...] = jnp.full(top.shape, NEG_BIG, jnp.float32)
    fetch(near_pieces(sc[0], *nears), kc, vc, [(q_all, q)], sems, lambda: clear(total, acc))
    transposed(sc, NEAR_TILES, vc, vt)

    @pl.loop(0, UNITS)
    def _(j):
        softmax_steps(sc, starts, q, NEAR_TILES, kc, vt, top, total, acc, j)


def forward_far(sc, starts, top0, total0, acc0, q_all, g_all, w_all, *refs):
    fars, (attn, norm, delta, left, right, kc, vc, vt, q, g, w, top, total, acc, sems) = refs[:3], refs[3:]
    weight = pltpu.make_async_copy(w_all, w, sems.at[13])
    weight.start()
    par, y, zl = sc[0], sc[1], sc[2]

    def meanwhile():
        top[...] = top0[...]
        total[...] = total0[...]
        acc[...] = acc0[...]

    fetch(far_pieces(par, *fars), kc, vc, [(q_all, q), (g_all, g)], sems, meanwhile)
    transposed(sc, FAR_TILES, vc, vt)

    @pl.loop(0, UNITS)
    def _(j):
        softmax_steps(sc, starts, q, FAR_TILES, kc, vt, top, total, acc, j)
        one = pl.ds(j, 1)
        out = acc[pl.ds(pl.multiple_of(j * HEAD, HEAD), HEAD), :] / total[one, :]
        norm[one, :] = top[one, :] + jnp.log2(total[one, :])
        g_unit = stacked(g, pl.multiple_of(j * UNIT, UNIT)).astype(jnp.float32).T
        delta[one, :] = jnp.sum(out * g_unit, axis=0, keepdims=True)
        flat = out.T.astype(jnp.bfloat16)
        for part in range(UNIT // BLOCK):
            number = j * (UNIT // BLOCK) + part
            place = 2 * ((number - y) & 3) + ((number >> 2) ^ zl)
            rows = pl.ds(pl.multiple_of(place * BLOCK, BLOCK), BLOCK)
            for h in range(HEADS_DEV):
                first = h * UNIT + part * BLOCK
                attn[rows, h * HEAD : (h + 1) * HEAD] = flat[first : first + BLOCK]

    weight.wait()
    cut = w.shape[1] // 2
    opposite = attn[4 * BLOCK : 6 * BLOCK, :]
    left[...] = dot(opposite, w[:, :cut]).astype(jnp.bfloat16)
    right[...] = dot(opposite, w[:, cut:]).astype(jnp.bfloat16)


def add_arrived(after, before, from_left, from_right, after_out, after_mine, before_out, before_mine):
    cut = from_left.shape[1]
    for rows, after_to, before_to in (
        (slice(0, BLOCK), after_mine, before_mine),
        (slice(BLOCK, 2 * BLOCK), after_out, before_out),
    ):
        there = after[rows, :cut].astype(jnp.float32) + from_left[rows, :].astype(jnp.float32)
        back = before[rows, cut:].astype(jnp.float32) + from_right[rows, :].astype(jnp.float32)
        after_to[:, :cut] = there.astype(jnp.bfloat16)
        after_to[:, cut:] = after[rows, cut:]
        before_to[:, :cut] = before[rows, :cut]
        before_to[:, cut:] = back.astype(jnp.bfloat16)


def gradient_steps(sc, starts, norm, delta, q, g, tiles, keys, kc, vc, kt, dk, dv, dq, j):
    row0 = pl.multiple_of(j * UNIT, UNIT)
    q_unit, g_unit = stacked(q, row0), stacked(g, row0)
    start, row = starts[pl.ds(j, 1), :], unit_rows(j)
    norm_unit, delta_unit = norm[pl.ds(j, 1), :], delta[pl.ds(j, 1), :]
    mine = pl.ds(pl.multiple_of(j * HEAD, HEAD), HEAD)

    def block(first_key, needs_mask):
        here = pl.ds(pl.multiple_of(first_key - tiles[0] * ROWS, keys), keys)
        s = dot(kc[here, :], q_unit, NT) * SCALE_LOG2
        if needs_mask:
            s = masked(s, first_key, start, row)
        p = jnp.exp2(s - norm_unit)
        dp = dot(vc[here, :], g_unit, NT)
        ds = (p * (dp - delta_unit)).astype(jnp.bfloat16)
        dk[here, :] += dot(ds, q_unit)
        dv[here, :] += dot(p.astype(jnp.bfloat16), g_unit)
        dq[mine, :] += dot(kt[:, here], ds)

    over_keys(sc, j, tiles, keys, block)


def tile_out(ref, dk, dv, slot):
    here = slice(slot * ROWS, (slot + 1) * ROWS)
    ref[0] = (dk[here, :] * SCALE).astype(jnp.bfloat16)
    ref[1] = dv[here, :].astype(jnp.bfloat16)


def clear(*refs):
    for ref in refs:
        ref[...] = jnp.zeros(ref.shape, jnp.float32)


def backward_before(sc, starts, norm, delta, attn, q_all, g_all, w_all, *refs):
    tiles, (dq, first, third, given, here, other, after, before, kc, vc, kt, q, g, w, dk, dv, sems) = refs[:5], refs[5:]
    weight = pltpu.make_async_copy(w_all, w, sems.at[13])
    weight.start()
    fetch(before_pieces(sc[0], *tiles), kc, vc, [(q_all, q), (g_all, g)], sems, lambda: clear(dq, dk, dv))
    transposed(sc, BEFORE_TILES, kc, kt)

    @pl.loop(0, UNITS)
    def _(j):
        gradient_steps(sc, starts, norm, delta, q, g, BEFORE_TILES, KEYS, kc, vc, kt, dk, dv, dq, j)

    tile_out(first, dk, dv, 0)
    tile_out(given.at[:2], dk, dv, 1)
    tile_out(third, dk, dv, 2)
    tile_out(given.at[2:], dk, dv, 3)
    weight.wait()
    for first_column in range(0, w.shape[1], 1024):
        part = slice(first_column, first_column + 1024)
        product = dot(attn[: 4 * BLOCK, :], w[:, part]).astype(jnp.bfloat16)
        here[:, part] = product[:BLOCK]
        other[:, part] = product[BLOCK : 2 * BLOCK]
        after[:, part] = product[2 * BLOCK :]
        before[:, part] = dot(attn[6 * BLOCK :, :], w[:, part]).astype(jnp.bfloat16)


def backward_own(sc, starts, norm, delta, dq0, q_all, g_all, own, gq, last, kc, vc, kt, q, g, dk, dv, dq, sems):
    def meanwhile():
        clear(dk, dv)
        dq[...] = dq0[...]

    fetch([(own, 0)], kc, vc, [(q_all, q), (g_all, g)], sems, meanwhile)
    transposed(sc, OWN_TILES, kc, kt)

    @pl.loop(0, UNITS)
    def _(j):
        gradient_steps(sc, starts, norm, delta, q, g, OWN_TILES, UNIT, kc, vc, kt, dk, dv, dq, j)
        flat = (dq[pl.ds(pl.multiple_of(j * HEAD, HEAD), HEAD), :] * SCALE).T.astype(jnp.bfloat16)
        row0 = pl.multiple_of(j * UNIT, UNIT)
        for h in range(HEADS_DEV):
            gq[pl.ds(row0, UNIT), h * HEAD : (h + 1) * HEAD] = flat[h * UNIT : (h + 1) * UNIT]

    tile_out(last, dk, dv, 0)


def pack(k, v, both):
    both[0] = k[...]
    both[1] = v[...]


VMEM = pl.BlockSpec(memory_space=pltpu.VMEM)
SMEM = pl.BlockSpec(memory_space=pltpu.SMEM)
ANY = pl.BlockSpec(memory_space=pl.ANY)
COST = pl.CostEstimate(flops=10**6, bytes_accessed=2**10, transcendentals=0)
TILE = (2, ROWS, HEAD)
STAT = (UNITS, COLS)
SUMS = (UNITS * HEAD, COLS)


def f32(shape):
    return jax.ShapeDtypeStruct(shape, jnp.float32)


def bf16(shape):
    return jax.ShapeDtypeStruct(shape, jnp.bfloat16)


def call(kernel, outs, dense, whole, tiles, scratch, slots):
    keys = pltpu.VMEM((slots * ROWS, HEAD), jnp.bfloat16)
    return pl.pallas_call(
        kernel,
        out_shape=outs,
        in_specs=[SMEM] + [VMEM] * (len(dense) - 1) + [ANY] * (len(whole) + len(tiles)),
        out_specs=[VMEM] * len(outs),
        scratch_shapes=[keys, keys, pltpu.VMEM((HEAD, (slots - 1) * ROWS), jnp.bfloat16)]
        + [pltpu.VMEM(array.shape, array.dtype) for array in whole]
        + [pltpu.VMEM(shape, jnp.float32) for shape in scratch]
        + [pltpu.SemaphoreType.DMA((14,))],
        compiler_params=pltpu.CompilerParams(vmem_limit_bytes=60 * 2**20),
        cost_estimate=COST,
        name=kernel.__name__,
    )(*dense, *whole, *tiles)


def shifted(x, distance):
    n = lax.axis_size("dp")
    return lax.ppermute(x, "dp", [(i, i + distance) for i in range(n) if 0 <= i + distance < n])


def twinned(x):
    return lax.ppermute(x, "dp", [(i, i ^ 1) for i in range(lax.axis_size("dp"))])


def along_y(x, step):
    return lax.ppermute(x, "tensor", [(i, (i & 4) | ((i + step) & 3)) for i in range(8)])


def across_z(x):
    return lax.ppermute(x, "tensor", [(i, i ^ 4) for i in range(8)])


def half(x):
    return x.astype(jnp.bfloat16)


def wide(x):
    return x.astype(jnp.float32)


def on_device(queries, key_rows, value_rows, grad_out, out_weight, lengths):
    dp, tensor = lax.axis_index("dp"), lax.axis_index("tensor")
    par = dp & 1
    odd = par == 1
    own = pl.pallas_call(pack, out_shape=bf16(TILE), name="pack")(key_rows, value_rows)
    near = shifted(own, 2)
    twin_own = twinned(own)
    far = shifted(own, 4)
    near_twin = twinned(near)

    base = (dp - REACH) * ROWS
    position = dp * ROWS + jnp.arange(ROWS, dtype=jnp.int32)
    ends = jnp.cumsum(lengths)
    start = jnp.max(jnp.where(ends[None, :] <= position[:, None], ends[None, :], 0), axis=1) - base
    start = start.reshape(UNITS, UNIT)
    head = jnp.stack([par, tensor & 3, tensor >> 2])
    sc = jnp.concatenate([head, start[:, 0], start[:, -1]]).astype(jnp.int32)
    starts = jnp.tile(start, (1, HEADS_DEV)).astype(jnp.int32)

    nears = (own, near, twin_own, near_twin)
    state = call(forward_near, (f32(STAT), f32(STAT), f32(SUMS)), (sc, starts), (queries,), nears, (), 4)
    far, state = lax.optimization_barrier((far, state))
    fars = (far, twinned(far), near_twin)
    sent = bf16((2 * BLOCK, out_weight.shape[1] // 2))
    attn, norm, delta, left, right = call(
        forward_far,
        (bf16(queries.shape), f32(STAT), f32(STAT), sent, sent),
        (sc, starts, *state),
        (queries, grad_out, out_weight),
        fars,
        (STAT, STAT, SUMS),
        3,
    )
    from_left, from_right = along_y(left, 1), along_y(right, -1)

    asked, whole = (sc, starts, norm, delta), (queries, grad_out)
    keys = (REACH * ROWS, HEAD)
    single, double = (bf16((n * BLOCK, out_weight.shape[1])) for n in (1, 2))
    dq, first, third, given, here, other, after, before = call(
        backward_before,
        (f32(SUMS), bf16(TILE), bf16(TILE), bf16((4, ROWS, HEAD)), single, single, double, double),
        (*asked, attn),
        (*whole, out_weight),
        (near, twin_own, near_twin, far, fars[1]),
        (keys, keys),
        REACH + 1,
    )
    from_left, from_right, dq, first, third, given, after, before = lax.optimization_barrier(
        (from_left, from_right, dq, first, third, given, after, before)
    )

    got = twinned(given)
    after, after_mine, before, before_mine = pl.pallas_call(
        add_arrived, out_shape=[single] * 4, cost_estimate=COST, name="add_arrived"
    )(after, before, from_left, from_right)
    from_left, from_right = along_y(after, 1), along_y(before, -1)
    far_sum = half(wide(first) + jnp.where(odd, wide(got[:2]), 0.0))
    near_sum = half(wide(third) + jnp.where(odd, wide(got[2:]), wide(got[:2])))
    far_sum, near_sum, dq = lax.optimization_barrier((far_sum, near_sum, dq))
    far_sum, near_sum = shifted(far_sum, -4), shifted(near_sum, -2)
    keys = (ROWS, HEAD)
    gq, last = call(
        backward_own, (bf16(queries.shape), bf16(TILE)), (*asked, dq), whole, (own,), (keys, keys, SUMS), 2
    )
    from_left, from_right, after_mine, before_mine, far_sum, near_sum, gq, last = lax.optimization_barrier(
        (from_left, from_right, after_mine, before_mine, far_sum, near_sum, gq, last)
    )
    other = half(wide(other) + wide(from_left) + wide(from_right))
    other, after_mine, before_mine = lax.optimization_barrier((other, after_mine, before_mine))
    from_left, from_right = along_y(after_mine, 1), along_y(before_mine, -1)
    other = across_z(other)
    own_sum = half(wide(last) + jnp.where(odd, 0.0, wide(got[2:])) + wide(near_sum) + wide(far_sum))
    projected = half(wide(here) + wide(from_left) + wide(from_right) + wide(other))
    return projected, gq, own_sum[0], own_sum[1]


def solution(mesh):
    split = P("dp", "tensor")
    return jax.shard_map(
        on_device,
        mesh=mesh,
        in_specs=(split, split, split, split, P("tensor", None), P()),
        out_specs=(P(("dp", "tensor"), None), split, split, split),
        check_vma=False,
    )
```
